256 devices in a mesh: dom: 32 (over x, z_lo, y), tile: 8 (over z_hi, core).
Axes of the slice: x: 4, y: 4, z: 8 (z_hi: 4, z_lo: 2; z = z_hi * 2 + z_lo), core: 2. Of those that a mesh axis runs over, the one named last changes fastest.
Arguments:
- cotangent: bfloat16 [25, 64, 655360], P(None, None, ('dom', 'tile')), may hold values from -0.59765625 to 0.59765625
- probe_pos: float32 [3, 655360], P(None, ('dom', 'tile')), may hold values from 0 to 160, as said below
- atom_pos: float32 [3, 32768], P(None, ('dom', 'tile')), may hold values from 0 to 160, as said below
- pair_tile: int32 [15360], P(('dom', 'tile')), may hold values from 0 to 19, as said below
- pair_block: int32 [15360], P(('dom', 'tile')), may hold values from 0 to 9, as said below
- pair_count: int32 [256], P(('dom', 'tile')), may hold values from 30 to 60, as said below
- send_left: int32 [32, 1], P('dom'), may hold values from 0 to 7, as said below
- send_right: int32 [32, 1], P('dom'), may hold values from 0 to 7, as said below
Outputs:
- atom_grad: bfloat16 [25, 64, 32768], P(None, None, ('dom', 'tile'))
The draws below stay inside these ranges and needn't reach their ends.
Inputs may be any that keep to these rules, and one draw needn't show every extreme that they name: `atom_pos`: atoms of slab s have x in [5 s, 5 s + 5]; those of its owned block b have y in [8 b, 8 b + 8]; z lies in [0, 32]. `probe_pos`: probes of device (s, t) have x in [5 s, 5 s + 5]; its local tile j, with k = j * 8 + t, has y in [8 * 8 * k / K, 8 * 8 * (k + 1) / K] where K = 160; z lies in [0, 32]. `pair_tile`: on each device the 60 slots hold distinct pairs of tile and block; each pairs a tile with a block whose y cell lies within two cells of the tile's. `pair_block`: on each device the 60 slots hold distinct pairs of tile and block. `pair_count`: some device uses all 60 slots. `send_left`: distinct within a slab's row. `send_right`: distinct within a slab's row.
All inputs are finite; a program needn't handle non-finite values.
Results may differ from the reference program's by a relative error of at most 0.0049.
Values sent between devices are 32-bit elements; how exact they have to be, the bound alone decides.
No kernel may reach another device: no remote copies, remote signals or barrier semaphores. Data moves between devices by JAX's collectives and lax.ppermute only.
A program may use at most 128 MiB of HBM per device.

```python
import jax
import jax.numpy as jnp
from jax import lax

C = 64
M = 25
AB_DOM = 8
GB = 1
PT = 20
NPAIR = 60
NB = 10
ATOMS = 32768
PROBES = 655360
N_DOM = 32
N_TILE = 8


slab_width = 5.0


cell_width = 8.0


depth_width = 32.0


def draw_atom_pos(key, part):
    key = jax.random.fold_in(key, 11)
    first, second, third = jax.random.split(key, 3)
    index = jnp.arange(ATOMS)
    per_slab = AB_DOM * 128
    domain = (index // per_slab).astype(jnp.float32)
    block = (index % per_slab // 128).astype(jnp.float32)
    frac = jax.random.uniform(first, (ATOMS,), jnp.float32)
    along = (domain + frac) * slab_width
    across = (block + jax.random.uniform(second, (ATOMS,), jnp.float32)) * cell_width
    depth = jax.random.uniform(third, (ATOMS,), jnp.float32) * depth_width
    return jnp.stack([along, across, depth])


def draw_probe_pos(key, part):
    key = jax.random.fold_in(key, 13)
    first, second, third = jax.random.split(key, 3)
    index = jnp.arange(PROBES)
    per_dev = PT * 128
    device = index // per_dev
    domain = (device // N_TILE).astype(jnp.float32)
    inside = device % N_TILE
    local_tile = index % per_dev // 128
    strip = (local_tile * N_TILE + inside).astype(jnp.float32)
    strips = float(PT * N_TILE)
    frac = jax.random.uniform(first, (PROBES,), jnp.float32)
    along = (domain + frac) * slab_width
    across = (strip + jax.random.uniform(second, (PROBES,), jnp.float32)) * (cell_width * AB_DOM / strips)
    depth = jax.random.uniform(third, (PROBES,), jnp.float32) * depth_width
    return jnp.stack([along, across, depth])


def lent_blocks(key, salt):
    keys = jax.random.split(jax.random.fold_in(key, salt), N_DOM)
    picks = jax.vmap(lambda k: jax.random.permutation(k, AB_DOM)[:GB])(keys)
    return picks.astype(jnp.int32)


def pair_combos(key):
    lefts = lent_blocks(key, 29)
    rights = lent_blocks(key, 31)
    devices = N_DOM * N_TILE
    dev_ids = jnp.arange(devices, dtype=jnp.int32)
    slab = dev_ids // N_TILE
    inside = dev_ids % N_TILE
    strip = jnp.arange(PT, dtype=jnp.int32)[None, :] * N_TILE + inside[:, None]
    strips = PT * N_TILE
    centre = (2 * strip + 1) * AB_DOM // (2 * strips)
    owned_ids = jnp.arange(AB_DOM, dtype=jnp.int32)
    own_near = jnp.abs(owned_ids[None, None, :] - centre[:, :, None]) <= 2
    left_ids = rights[(slab - 1) % N_DOM]
    right_ids = lefts[(slab + 1) % N_DOM]
    left_near = jnp.abs(left_ids[:, None, :] - centre[:, :, None]) <= 2
    right_near = jnp.abs(right_ids[:, None, :] - centre[:, :, None]) <= 2
    near = jnp.concatenate([own_near, left_near, right_near], axis=2).reshape(devices, PT * NB)
    keys = jax.random.split(jax.random.fold_in(key, 37), devices)
    perms = jax.vmap(lambda k: jax.random.permutation(k, PT * NB))(keys).astype(jnp.int32)
    scores = perms + near.astype(jnp.int32) * (PT * NB)
    values, picks = lax.top_k(scores, NPAIR)
    return picks.reshape(-1).astype(jnp.int32)


def draw_pair_tile(key, part):
    combos = pair_combos(key)
    key = jax.random.fold_in(key, 17)
    return combos // NB


def draw_pair_block(key, part):
    combos = pair_combos(key)
    key = jax.random.fold_in(key, 19)
    return combos % NB


def draw_pair_count(key, part):
    key = jax.random.fold_in(key, 23)
    first, second = jax.random.split(key)
    counts = jax.random.randint(first, (N_DOM * N_TILE,), NPAIR // 2, NPAIR + 1)
    busiest = jax.random.randint(second, (), 0, N_DOM * N_TILE)
    return counts.at[busiest].set(NPAIR).astype(jnp.int32)


def draw_send_left(key, part):
    values = lent_blocks(key, 29)
    key = jax.random.fold_in(key, 41)
    return values


def draw_send_right(key, part):
    values = lent_blocks(key, 31)
    key = jax.random.fold_in(key, 43)
    return values


def steps_of(stream_key, shape, cuts, low, high):
    level, own = 1.0, jax.random.fold_in(stream_key, 6)
    for position, blocks in cuts:
        draws = jnp.exp(jax.random.uniform(jax.random.fold_in(own, position), (blocks,), jnp.float32, low / len(cuts), high / len(cuts)))
        level = level * jnp.repeat(draws, shape[position] // blocks).reshape([-1 if axis == position else 1 for axis in range(len(shape))])
    return level


def scatter_about(key, shape, scale, reach, pieces=(), kind=jnp.bfloat16):
    factor_of = steps_of(key, shape, pieces, -0.22, 0.18) if pieces else 1.0
    values = jax.random.normal(key, shape, jnp.float32) * scale * factor_of
    return jnp.minimum(jnp.maximum(values, -reach), reach).astype(kind)


def setup_inputs(seed: int = 0) -> dict:
    splits = jax.random.split(jax.random.key(seed), 9)
    cotangent = scatter_about(splits[0], (M, C, PROBES), 0.1, 0.59765625, ((2, 256),))
    probe_pos = draw_probe_pos(jax.random.fold_in(splits[8], 71), 0)
    atom_pos = draw_atom_pos(jax.random.fold_in(splits[8], 71), 0)
    pair_tile = draw_pair_tile(jax.random.fold_in(splits[8], 71), 0)
    pair_block = draw_pair_block(jax.random.fold_in(splits[8], 71), 0)
    pair_count = draw_pair_count(jax.random.fold_in(splits[8], 71), 0)
    send_left = draw_send_left(jax.random.fold_in(splits[8], 71), 0)
    send_right = draw_send_right(jax.random.fold_in(splits[8], 71), 0)
    return dict(cotangent=cotangent, probe_pos=probe_pos, atom_pos=atom_pos, pair_tile=pair_tile, pair_block=pair_block, pair_count=pair_count, send_left=send_left, send_right=send_right)


cutoff = 4.0
slab_width = 5.0
block_rows = 128


def harmonics(x, y, z):
    xx = x * x
    yy = y * y
    zz = z * z
    rr = xx + yy + zz
    rows = [jnp.ones_like(x),
            2.0 * x, 2.0 * y, 2.0 * z,
            3.0 * x * y, 3.0 * y * z, 1.5 * (3.0 * zz - rr), 3.0 * x * z, 1.5 * (xx - yy),
            5.0 * y * (3.0 * xx - yy), 10.0 * x * y * z, 5.0 * y * (5.0 * zz - rr), 5.0 * z * (5.0 * zz - 3.0 * rr),
            5.0 * x * (5.0 * zz - rr), 5.0 * z * (xx - yy), 5.0 * x * (xx - 3.0 * yy),
            8.0 * x * y * (xx - yy), 8.0 * y * z * (3.0 * xx - yy), 8.0 * x * y * (7.0 * zz - rr),
            8.0 * y * z * (7.0 * zz - 3.0 * rr), 35.0 * zz * zz - 30.0 * zz * rr + 3.0 * rr * rr,
            8.0 * x * z * (7.0 * zz - 3.0 * rr), 4.0 * (xx - yy) * (7.0 * zz - rr), 8.0 * x * z * (xx - 3.0 * yy),
            2.0 * (xx * xx - 6.0 * xx * yy + yy * yy)]
    return jnp.stack(rows)


def geometry(probe, atom):
    delta = (probe[:, :, None] - atom[:, None, :]) / cutoff
    sq = delta[0] * delta[0] + delta[1] * delta[1] + delta[2] * delta[2]
    envelope = jnp.where(sq < 1.0, (1.0 - sq) * (1.0 - sq), 0.0)
    return (envelope[None] * harmonics(delta[0], delta[1], delta[2])).astype(jnp.bfloat16)


def reference(cotangent, probe_pos, atom_pos, pair_tile, pair_block, pair_count, send_left, send_right):
    ndom = N_DOM
    ntile = N_TILE
    span = AB_DOM * block_rows
    box = ndom * slab_width
    own_pos = atom_pos.reshape(3, ndom, AB_DOM, block_rows)
    owned_ids = jnp.arange(AB_DOM).astype(jnp.int32)
    left_hot = (send_left[:, :, None] == owned_ids[None, None, :]).astype(jnp.float32)
    right_hot = (send_right[:, :, None] == owned_ids[None, None, :]).astype(jnp.float32)
    sent_left = jnp.einsum('dgb,kdbi->dkgi', left_hot, own_pos, precision=lax.Precision.HIGHEST)
    sent_right = jnp.einsum('dgb,kdbi->dkgi', right_hot, own_pos, precision=lax.Precision.HIGHEST)
    dom_ids = jnp.arange(ndom).astype(jnp.int32)
    left_ghost = jnp.roll(sent_right, 1, axis=0)
    left_ghost = left_ghost.at[:, 0].add(jnp.where(dom_ids == 0, -box, 0.0)[:, None, None])
    right_ghost = jnp.roll(sent_left, -1, axis=0)
    right_ghost = right_ghost.at[:, 0].add(jnp.where(dom_ids == ndom - 1, box, 0.0)[:, None, None])
    table_pos = jnp.concatenate([own_pos.transpose(1, 0, 2, 3), left_ghost, right_ghost], axis=2)
    table_pos = table_pos.reshape(ndom, 3, NB * block_rows)
    width = PT * block_rows

    def one_domain(dom):
        tpos = table_pos[dom]

        def one_device(t, table):
            dev = (dom * ntile + t).astype(jnp.int32)
            grads = lax.dynamic_slice_in_dim(cotangent, dev * width, width, 2)
            ppos = lax.dynamic_slice_in_dim(probe_pos, dev * width, width, 1)
            tiles = lax.dynamic_slice_in_dim(pair_tile, dev * NPAIR, NPAIR, 0)
            blocks = lax.dynamic_slice_in_dim(pair_block, dev * NPAIR, NPAIR, 0)

            def one_pair(j, acc):
                tile = tiles[j].astype(jnp.int32)
                block = blocks[j].astype(jnp.int32)
                probe = lax.dynamic_slice_in_dim(ppos, tile * block_rows, block_rows, 1)
                atom = lax.dynamic_slice_in_dim(tpos, block * block_rows, block_rows, 1)
                geom = geometry(probe, atom)
                piece = lax.dynamic_slice_in_dim(grads, tile * block_rows, block_rows, 2)
                term = jnp.einsum('mcp,mpa->mca', piece.astype(jnp.float32), geom.astype(jnp.float32))
                old = lax.dynamic_slice_in_dim(acc, block * block_rows, block_rows, 2)
                return lax.dynamic_update_slice_in_dim(acc, old + term, block * block_rows, 2)

            return lax.fori_loop(0, pair_count[dev], one_pair, table)

        return lax.fori_loop(0, ntile, one_device, jnp.zeros((M, C, NB * block_rows), jnp.float32))

    tables = lax.map(one_domain, dom_ids)
    own = tables[..., :span].reshape(ndom, M, C, AB_DOM, block_rows)
    left_part = tables[..., span:span + GB * block_rows]
    right_part = tables[..., span + GB * block_rows:]
    from_left = jnp.roll(right_part, 1, axis=0).reshape(ndom, M, C, GB, block_rows)
    from_right = jnp.roll(left_part, -1, axis=0).reshape(ndom, M, C, GB, block_rows)
    added = jnp.einsum('dgb,dmcgi->dmcbi', left_hot, from_left, precision=lax.Precision.HIGHEST)
    added = added + jnp.einsum('dgb,dmcgi->dmcbi', right_hot, from_right, precision=lax.Precision.HIGHEST)
    total = (own + added).reshape(ndom, M, C, span).transpose(1, 2, 0, 3).reshape(M, C, ndom * span)
    return total.astype(jnp.bfloat16)
```

```python
import functools

import jax
import jax.numpy as jnp
from jax import lax
from jax.experimental import pallas as pl
from jax.experimental.pallas import tpu as pltpu
from jax.sharding import PartitionSpec as P

cutoff = 4.0
slab_width = 5.0
rows = 128
offsets = (2, 1, 3, 0)
tiles_max = 20
every = tuple(range(25))


def harmonics(e, x, y, z, xx, yy, zz, wanted):
    rr = xx + yy + zz
    ex = e * x
    ey = e * y
    ez = e * z
    exy = ex * y
    eyz = ey * z
    exz = ex * z
    d = xx - yy
    ed = e * d
    z3 = 3.0 * zz
    z5 = 5.0 * zz
    z7 = 7.0 * zz
    r3 = 3.0 * rr
    f = 3.0 * xx - yy
    k = xx - 3.0 * yy
    g = z5 - rr
    h = z5 - r3
    w = z7 - rr
    v = z7 - r3
    made = {
        0: lambda: e,
        1: lambda: 2.0 * ex,
        2: lambda: 2.0 * ey,
        3: lambda: 2.0 * ez,
        4: lambda: 3.0 * exy,
        5: lambda: 3.0 * eyz,
        6: lambda: (1.5 * e) * (z3 - rr),
        7: lambda: 3.0 * exz,
        8: lambda: 1.5 * ed,
        9: lambda: (5.0 * ey) * f,
        10: lambda: 10.0 * (exy * z),
        11: lambda: (5.0 * ey) * g,
        12: lambda: (5.0 * ez) * h,
        13: lambda: (5.0 * ex) * g,
        14: lambda: (5.0 * ez) * d,
        15: lambda: (5.0 * ex) * k,
        16: lambda: (8.0 * exy) * d,
        17: lambda: (8.0 * eyz) * f,
        18: lambda: (8.0 * exy) * w,
        19: lambda: (8.0 * eyz) * v,
        20: lambda: e * (z5 * (z7 - 6.0 * rr) + r3 * rr),
        21: lambda: (8.0 * exz) * v,
        22: lambda: (4.0 * ed) * w,
        23: lambda: (8.0 * exz) * k,
        24: lambda: (2.0 * e) * (xx * k - yy * f),
    }
    return [made[m]() for m in wanted]


far = 1000.0
chunk = 16


def geometry(tile, r, atom, probe_ref):
    p = probe_ref[pl.ds(pl.multiple_of(tile * rows + r * chunk, chunk), chunk), :]
    x = p[:, 0:1] - atom[0]
    y = p[:, 1:2] - atom[1]
    z = p[:, 2:3] - atom[2]
    xx = x * x
    yy = y * y
    zz = z * z
    inside = jnp.maximum(1.0 - (xx + yy + zz), 0.0)
    return harmonics(inside * inside, x, y, z, xx, yy, zz, every)


def add_term(m, side, tiles, cot_ref, geom, top_ref, bottom_ref):
    piece = jnp.concatenate(
        [cot_ref[m, :, pl.ds(pl.multiple_of(tile * rows, rows), rows)] for tile in tiles], axis=1
    )
    term = jnp.dot(piece, geom[m], preferred_element_type=jnp.float32)
    half = term.shape[0] // 2
    at = slice(m * half, m * half + half)
    top_ref[side, at, :] = top_ref[side, at, :] + term[:half]
    bottom_ref[side, at, :] = bottom_ref[side, at, :] + term[half:]


def make_and_add(make, add, atoms, probe_ref, cot_ref, made, used, outs):
    chunks = [(n, r) for n in range(2) for r in range(rows // chunk)] if make else []
    turns = len(chunks) or 1
    for turn in range(turns):
        if make:
            n, r = chunks[turn]
            values = geometry(make[n], r, atoms[n], probe_ref)
            at = slice(n * rows + r * chunk, n * rows + r * chunk + chunk)
            for m, value in enumerate(values):
                made[m, at, :] = value.astype(jnp.bfloat16)
        if add:
            side, tiles = add
            for m in range(turn * len(every) // turns, (turn + 1) * len(every) // turns):
                add_term(m, side, tiles, cot_ref, used, *outs)


def fill_lists(slots, tile_ref, block_ref, count, lists, counts):
    def clear(b, carry):
        counts[b] = 0
        return carry

    lax.fori_loop(0, 10, clear, 0)

    def put(j, carry):
        b = block_ref[j]
        n = counts[b]
        lists[b * tiles_max + n] = tile_ref[j]
        counts[b] = n + 1
        return carry

    lax.fori_loop(0, jnp.minimum(count, slots), put, 0)


def list_steps(side, b, atom, bounds, lists, counts, steps, n):
    ymin = jnp.min(atom[1])
    ymax = jnp.max(atom[1])

    def keep(j, found):
        tile = lists[b * tiles_max + j]
        gap = jnp.maximum(ymin - bounds[1, tile], bounds[0, tile] - ymax)
        near = gap < 1.0
        at = 3 * n + 3 * (found // 2)
        odd = found % 2

        @pl.when(near)
        def _():
            steps[at] = side
            steps[at + 1 + odd] = tile

            @pl.when(odd == 0)
            def _():
                steps[at + 2] = -1

        return found + jnp.where(near, 1, 0)

    return n + (lax.fori_loop(0, counts[b], keep, 0) + 1) // 2


def kernel(kind, slots, box, meta, tile_ref, block_ref, bounds, probe_ref, pos_ref, cot_ref, after_ref, *rest):
    *outs, first_geom, second_geom, atom_ref, lists, counts, steps = rest
    step = pl.program_id(0)

    @pl.when(step == 0)
    def _():
        fill_lists(slots, tile_ref, block_ref, meta[0], lists, counts)

    core = meta[2]
    if kind == "main":
        halves = [ref.at[0] for ref in outs]
    else:
        halves = [outs[0].at[0], outs[0].at[1]]
    for ref in halves:
        ref[...] = jnp.zeros(ref.shape, jnp.float32)
    n = 0
    for side in range(2):
        if kind == "main":
            offset = jnp.where(step == 0, 2, jnp.where(step == 1, 1, jnp.where(step == 2, 3, 0)))
            chip = lax.rem(meta[1] + offset, 4)
            b = chip * 2 + (core if side == 0 else 1 - core)
            place = lax.bitwise_xor(chip, meta[1])
            atom = [pos_ref[place, side, i : i + 1, :] for i in range(3)]
        else:
            which = core if side == 0 else 1 - core
            b = 8 + which
            lent_left = jnp.max(pos_ref[0, 0, 9:10, :])
            lent_right = jnp.max(pos_ref[0, 0, 13:14, :])
            source = jnp.where(which == 0, lent_left, lent_right).astype(jnp.int32)
            place = lax.bitwise_xor(source // 2, meta[1])
            other = jnp.where(lax.rem(source, 2) == core, 0, 1)
            left = [pos_ref[place, other, 5 + i : 6 + i, :] for i in range(3)]
            right = [pos_ref[place, other, 10 + i : 11 + i, :] for i in range(3)]
            left[0] = left[0] + jnp.where(meta[3] == 0, -box, 0.0)
            right[0] = right[0] + jnp.where(meta[3] == meta[4] - 1, box, 0.0)
            atom = [jnp.where(which == 0, l, r) for l, r in zip(left, right)]
        atom = [a * 0.25 for a in atom]
        for i in range(3):
            atom_ref[side, i : i + 1, :] = atom[i]
        n = list_steps(side, b, atom, bounds, lists, counts, steps, n)

    def one(j):
        side, first, second = steps[3 * j], steps[3 * j + 1], steps[3 * j + 2]
        atom = [atom_ref[side, i : i + 1, :] for i in range(3)]
        moved = [atom[0] - jnp.where(second < 0, far, 0.0), *atom[1:]]
        return side, (first, jnp.maximum(second, 0)), (atom, moved)

    def turn(make, add, made, used):
        made_step = one(make) if make is not None else (None, None, None)
        added = one(add)[:2] if add is not None else None
        make_and_add(made_step[1], added, made_step[2], probe_ref, cot_ref, made, used, halves)

    @pl.when(n > 0)
    def _():
        turn(0, None, first_geom, None)

    def both(k, carry):
        turn(2 * k + 1, 2 * k, second_geom, first_geom)
        turn(2 * k + 2, 2 * k + 1, first_geom, second_geom)
        return carry

    whole = jnp.maximum(n - 1, 0) // 2
    lax.fori_loop(0, whole, both, 0)

    @pl.when(n - 2 * whole == 1)
    def _():
        turn(None, n - 1, None, first_geom)

    @pl.when(n - 2 * whole == 2)
    def _():
        turn(n - 1, n - 2, second_geom, first_geom)
        turn(None, n - 1, None, second_geom)


def compute(kind, meta, pair_tile, pair_block, bounds, probe, pos, cot, box, after):
    harm, chan, width = cot.shape
    height = harm * chan // 2
    slots = pair_tile.shape[0]
    smem = pl.BlockSpec(memory_space=pltpu.SMEM)
    whole = pl.BlockSpec(memory_space=pltpu.VMEM)
    any_space = pl.BlockSpec(memory_space=pl.ANY)
    if kind == "main":
        grid = 4
        shape = [jax.ShapeDtypeStruct((4, 2, height, rows), jnp.float32)] * 2
        out_specs = [
            pl.BlockSpec((1, 2, height, rows), lambda i: (jnp.where(i == 1, 2, jnp.where(i == 2, 1, i)), 0, 0, 0)),
            pl.BlockSpec((1, 2, height, rows), lambda i: (i, 0, 0, 0)),
        ]
    else:
        grid = 1
        shape = [jax.ShapeDtypeStruct((2, 2, height, rows), jnp.float32)]
        out_specs = [pl.BlockSpec((2, 2, height, rows), lambda i: (0, 0, 0, 0))]
    geom = pltpu.VMEM((harm, 2 * rows, rows), jnp.bfloat16)
    return pl.pallas_call(
        functools.partial(kernel, kind, slots, box),
        out_shape=shape,
        grid=(grid,),
        in_specs=[smem, smem, smem, smem, whole, whole, whole, any_space],
        out_specs=out_specs,
        scratch_shapes=[
            geom,
            geom,
            pltpu.VMEM((2, 8, rows), jnp.float32),
            pltpu.SMEM((10 * tiles_max,), jnp.int32),
            pltpu.SMEM((16,), jnp.int32),
            pltpu.SMEM((3 * (2 * tiles_max + 4),), jnp.int32),
        ],
        compiler_params=pltpu.CompilerParams(vmem_limit_bytes=24 * 1024 * 1024),
        cost_estimate=pl.CostEstimate(flops=0, bytes_accessed=0, transcendentals=0),
        name=kind,
    )(meta, pair_tile, pair_block, bounds, probe, pos, cot, after)


def hold_kernel(cot_hbm, probe_ref, bounds_ref, meta_ref, out_ref, token_ref, sem):
    copy = pltpu.make_async_copy(cot_hbm, out_ref, sem)
    copy.start()
    token_ref[...] = jnp.zeros_like(token_ref)
    copy.wait()


def hold(cot, probe, bounds, meta):
    any_space = pl.BlockSpec(memory_space=pl.ANY)
    whole = pl.BlockSpec(memory_space=pltpu.VMEM)
    return pl.pallas_call(
        hold_kernel,
        out_shape=[
            pltpu.VMEM(cot.shape, cot.dtype),
            jax.ShapeDtypeStruct((15, rows), jnp.float32),
        ],
        in_specs=[pl.BlockSpec(memory_space=pltpu.HBM), any_space, any_space, any_space],
        out_specs=[whole, whole],
        scratch_shapes=[pltpu.SemaphoreType.DMA],
        compiler_params=pltpu.CompilerParams(vmem_limit_bytes=16 * 1024 * 1024),
        name="hold",
    )(pltpu.with_memory_space_constraint(cot, pltpu.HBM), probe, bounds, meta)


def on_device(
    cotangent, probe_pos, atom_pos, pair_tile, pair_block, pair_count, send_left, send_right
):
    ndom = lax.axis_size("dom")
    ntile = lax.axis_size("tile")
    slab = lax.axis_index("dom")
    place = lax.axis_index("tile")
    core = place % 2
    chips = ntile // 2
    box = ndom * slab_width
    up = [(i, (i + 1) % ndom) for i in range(ndom)]
    down = [(j, i) for i, j in up]
    swap = [(i, i ^ 1) for i in range(ntile)]

    def along(o):
        return [(z * 2 + c, ((z + o) % chips) * 2 + c) for z in range(chips) for c in range(2)]

    ids = jnp.concatenate([send_left, send_right], axis=0)[:, :1].astype(jnp.float32)
    own = jnp.concatenate([atom_pos, jnp.broadcast_to(ids, (2, rows))], axis=0)
    own = lax.optimization_barrier(own)
    before = lax.ppermute(own, "dom", up)
    after = lax.ppermute(own, "dom", down)
    meta = jnp.stack([pair_count[0], place // 2, core, slab, jnp.int32(ndom)])
    shaped = (probe_pos[1] * 0.25).reshape(-1, rows)
    bounds = jnp.stack([jnp.min(shaped, axis=1), jnp.max(shaped, axis=1)])
    probe = (probe_pos * 0.25).T
    cot, token = hold(cotangent, probe, bounds, meta)
    three = jnp.concatenate([own, before, after], axis=0)
    three = three + token
    pos = three[None]
    for bit in (1, 2, 4):
        other = lax.ppermute(pos, "tile", [(i, i ^ bit) for i in range(ntile)])
        pos = jnp.concatenate([pos, other], axis=0)
    pos = pos.reshape(chips, 2, *three.shape)

    home = []
    for s in range(ndom):
        for t in range(ntile):
            way = 1 if t % 2 else -1
            home.append((s * ntile + t, ((s + way) % ndom) * ntile + t))
    lent_id = jnp.where(core == 0, send_right[0, 0], send_left[0, 0])
    owner = [(place // 2 + o) % chips * 2 for o in offsets]
    is_keep = [o + core == lent_id for o in owner]
    is_send = [o + 1 - core == lent_id for o in owner]

    args = (meta, pair_tile, pair_block, bounds, probe, pos, cot, box)
    (lent,) = compute("lent", *args, atom_pos)
    lent = lent[:, 0] + lax.ppermute(lent[:, 1], "tile", swap)
    back = lax.ppermute(lent, ("dom", "tile"), home)
    top, bottom = compute("main", *args, lent)

    def over_cores(part, half, first, blocks):
        at = slice(first, first + 2)
        second = lax.broadcasted_iota(jnp.int32, (2, 1, 1), 0) == 1
        two = jnp.where(second, is_send[blocks[1]], is_send[blocks[0]])
        send = part[at, 1] + jnp.where(two, back[half], 0.0)
        got = lax.ppermute(send, "tile", swap)
        return [
            part[first + i, 0] + jnp.where(is_keep[n], back[half], 0.0) + got[i]
            for i, n in enumerate(blocks)
        ]

    far_top, last_top = over_cores(top, 0, 0, (0, 2))
    far_bottom, next_bottom = over_cores(bottom, 1, 0, (0, 1))
    far_ahead = lax.ppermute(far_top, "tile", along(1))
    far_behind = lax.ppermute(far_bottom, "tile", along(-1))
    near_behind = lax.ppermute(last_top, "tile", along(-1))
    near_ahead = lax.ppermute(next_bottom, "tile", along(1))
    next_top, here_top = over_cores(top, 0, 2, (1, 3))
    last_bottom, here_bottom = over_cores(bottom, 1, 2, (2, 3))
    sums = lax.optimization_barrier((next_top + far_ahead, last_bottom + far_behind))
    end_ahead = lax.ppermute(sums[0], "tile", along(1))
    end_behind = lax.ppermute(sums[1], "tile", along(-1))
    halves = (here_top + near_behind + end_ahead, here_bottom + near_ahead + end_behind)
    shape = (cotangent.shape[0], -1, rows)
    total = jnp.concatenate([h.astype(jnp.bfloat16).reshape(shape) for h in halves], axis=1)
    return total


def solution(mesh):
    placed = (
        P(None, None, ("dom", "tile")),
        P(None, ("dom", "tile")),
        P(None, ("dom", "tile")),
        P(("dom", "tile")),
        P(("dom", "tile")),
        P(("dom", "tile")),
        P("dom", None),
        P("dom", None),
    )
    return jax.shard_map(
        on_device,
        mesh=mesh,
        in_specs=placed,
        out_specs=P(None, None, ("dom", "tile")),
        check_vma=False,
    )
```

```python
import functools

import jax
import jax.numpy as jnp
from jax import lax
from jax.experimental import pallas as pl
from jax.experimental.pallas import tpu as pltpu
from jax.sharding import PartitionSpec as P

cutoff = 4.0
slab_width = 5.0
rows = 128
offsets = (2, 1, 3, 0)
tiles_max = 20
every = tuple(range(25))


def harmonics(e, x, y, z, xx, yy, zz, wanted):
    rr = xx + yy + zz
    ex = e * x
    ey = e * y
    ez = e * z
    exy = ex * y
    eyz = ey * z
    exz = ex * z
    d = xx - yy
    ed = e * d
    z3 = 3.0 * zz
    z5 = 5.0 * zz
    z7 = 7.0 * zz
    r3 = 3.0 * rr
    f = 3.0 * xx - yy
    k = xx - 3.0 * yy
    g = z5 - rr
    h = z5 - r3
    w = z7 - rr
    v = z7 - r3
    made = {
        0: lambda: e,
        1: lambda: 2.0 * ex,
        2: lambda: 2.0 * ey,
        3: lambda: 2.0 * ez,
        4: lambda: 3.0 * exy,
        5: lambda: 3.0 * eyz,
        6: lambda: (1.5 * e) * (z3 - rr),
        7: lambda: 3.0 * exz,
        8: lambda: 1.5 * ed,
        9: lambda: (5.0 * ey) * f,
        10: lambda: 10.0 * (exy * z),
        11: lambda: (5.0 * ey) * g,
        12: lambda: (5.0 * ez) * h,
        13: lambda: (5.0 * ex) * g,
        14: lambda: (5.0 * ez) * d,
        15: lambda: (5.0 * ex) * k,
        16: lambda: (8.0 * exy) * d,
        17: lambda: (8.0 * eyz) * f,
        18: lambda: (8.0 * exy) * w,
        19: lambda: (8.0 * eyz) * v,
        20: lambda: e * (z5 * (z7 - 6.0 * rr) + r3 * rr),
        21: lambda: (8.0 * exz) * v,
        22: lambda: (4.0 * ed) * w,
        23: lambda: (8.0 * exz) * k,
        24: lambda: (2.0 * e) * (xx * k - yy * f),
    }
    return [made[m]() for m in wanted]


far = 1000.0
chunk = 16


def geometry(tile, r, atom, probe_ref):
    p = probe_ref[pl.ds(pl.multiple_of(tile * rows + r * chunk, chunk), chunk), :]
    x = p[:, 0:1] - atom[0]
    y = p[:, 1:2] - atom[1]
    z = p[:, 2:3] - atom[2]
    xx = x * x
    yy = y * y
    zz = z * z
    inside = jnp.maximum(1.0 - (xx + yy + zz), 0.0)
    return harmonics(inside * inside, x, y, z, xx, yy, zz, every)


def add_term(m, side, tiles, cot_ref, geom, top_ref, bottom_ref):
    piece = jnp.concatenate(
        [cot_ref[m, :, pl.ds(pl.multiple_of(tile * rows, rows), rows)] for tile in tiles], axis=1
    )
    term = jnp.dot(piece, geom[m], preferred_element_type=jnp.float32)
    half = term.shape[0] // 2
    at = slice(m * half, m * half + half)
    top_ref[side, at, :] = top_ref[side, at, :] + term[:half]
    bottom_ref[side, at, :] = bottom_ref[side, at, :] + term[half:]


def make_and_add(make, add, atoms, probe_ref, cot_ref, made, used, outs):
    chunks = [(n, r) for n in range(2) for r in range(rows // chunk)] if make else []
    turns = len(chunks) or 1
    for turn in range(turns):
        if make:
            n, r = chunks[turn]
            values = geometry(make[n], r, atoms[n], probe_ref)
            at = slice(n * rows + r * chunk, n * rows + r * chunk + chunk)
            for m, value in enumerate(values):
                made[m, at, :] = value.astype(jnp.bfloat16)
        if add:
            side, tiles = add
            for m in range(turn * len(every) // turns, (turn + 1) * len(every) // turns):
                add_term(m, side, tiles, cot_ref, used, *outs)


def fill_lists(slots, tile_ref, block_ref, count, lists, counts):
    def clear(b, carry):
        counts[b] = 0
        return carry

    lax.fori_loop(0, 10, clear, 0)

    def put(j, carry):
        b = block_ref[j]
        n = counts[b]
        lists[b * tiles_max + n] = tile_ref[j]
        counts[b] = n + 1
        return carry

    lax.fori_loop(0, jnp.minimum(count, slots), put, 0)


def list_steps(side, b, atom, bounds, lists, counts, steps, n):
    ymin = jnp.min(atom[1])
    ymax = jnp.max(atom[1])

    def keep(j, found):
        tile = lists[b * tiles_max + j]
        gap = jnp.maximum(ymin - bounds[1, tile], bounds[0, tile] - ymax)
        near = gap < 1.0
        at = 3 * n + 3 * (found // 2)
        odd = found % 2

        @pl.when(near)
        def _():
            steps[at] = side
            steps[at + 1 + odd] = tile

            @pl.when(odd == 0)
            def _():
                steps[at + 2] = -1

        return found + jnp.where(near, 1, 0)

    return n + (lax.fori_loop(0, counts[b], keep, 0) + 1) // 2


def kernel(kind, slots, box, meta, tile_ref, block_ref, bounds, probe_ref, pos_ref, cot_ref, after_ref, *rest):
    *outs, first_geom, second_geom, atom_ref, lists, counts, steps = rest[: len(rest) - 2 * (kind == "main")]
    step = pl.program_id(0)
    if kind == "main":
        held, sem = rest[-2:]
        copy = pltpu.make_async_copy(cot_ref, held, sem)
        cot_ref = held

    @pl.when(step == 0)
    def _():
        if kind == "main":
            copy.start()
        fill_lists(slots, tile_ref, block_ref, meta[0], lists, counts)

    core = meta[2]
    if kind == "main":
        halves = [ref.at[:, 0] for ref in outs]
    else:
        halves = [outs[0].at[0], outs[0].at[1]]
    for ref in halves:
        ref[...] = jnp.zeros(ref.shape, jnp.float32)
    n = 0
    for side in range(2):
        if kind == "main":
            offset = jnp.where(step == 0, 2, jnp.where(step == 1, 1, jnp.where(step == 2, 3, 0)))
            chip = lax.rem(meta[1] + offset, 4)
            b = chip * 2 + (core if side == 0 else 1 - core)
            place = lax.bitwise_xor(chip, meta[1])
            atom = [pos_ref[place, side, i : i + 1, :] for i in range(3)]
        else:
            which = core if side == 0 else 1 - core
            b = 8 + which
            lent_left = jnp.max(pos_ref[0, 0, 9:10, :])
            lent_right = jnp.max(pos_ref[0, 0, 13:14, :])
            source = jnp.where(which == 0, lent_left, lent_right).astype(jnp.int32)
            place = lax.bitwise_xor(source // 2, meta[1])
            other = jnp.where(lax.rem(source, 2) == core, 0, 1)
            left = [pos_ref[place, other, 5 + i : 6 + i, :] for i in range(3)]
            right = [pos_ref[place, other, 10 + i : 11 + i, :] for i in range(3)]
            left[0] = left[0] + jnp.where(meta[3] == 0, -box, 0.0)
            right[0] = right[0] + jnp.where(meta[3] == meta[4] - 1, box, 0.0)
            atom = [jnp.where(which == 0, l, r) for l, r in zip(left, right)]
        atom = [a * 0.25 for a in atom]
        for i in range(3):
            atom_ref[side, i : i + 1, :] = atom[i]
        n = list_steps(side, b, atom, bounds, lists, counts, steps, n)

    def one(j):
        side, first, second = steps[3 * j], steps[3 * j + 1], steps[3 * j + 2]
        atom = [atom_ref[side, i : i + 1, :] for i in range(3)]
        moved = [atom[0] - jnp.where(second < 0, far, 0.0), *atom[1:]]
        return side, (first, jnp.maximum(second, 0)), (atom, moved)

    def turn(make, add, made, used):
        made_step = one(make) if make is not None else (None, None, None)
        added = one(add)[:2] if add is not None else None
        make_and_add(made_step[1], added, made_step[2], probe_ref, cot_ref, made, used, halves)

    @pl.when(n > 0)
    def _():
        turn(0, None, first_geom, None)

    if kind == "main":
        pl.when(step == 0)(copy.wait)

    def both(k, carry):
        turn(2 * k + 1, 2 * k, second_geom, first_geom)
        turn(2 * k + 2, 2 * k + 1, first_geom, second_geom)
        return carry

    whole = jnp.maximum(n - 1, 0) // 2
    lax.fori_loop(0, whole, both, 0)

    @pl.when(n - 2 * whole == 1)
    def _():
        turn(None, n - 1, None, first_geom)

    @pl.when(n - 2 * whole == 2)
    def _():
        turn(n - 1, n - 2, second_geom, first_geom)
        turn(None, n - 1, None, second_geom)


def compute(kind, meta, pair_tile, pair_block, bounds, probe, pos, cot, box, after):
    harm, chan, width = cot.shape
    height = harm * chan // 2
    slots = pair_tile.shape[0]
    smem = pl.BlockSpec(memory_space=pltpu.SMEM)
    whole = pl.BlockSpec(memory_space=pltpu.VMEM)
    any_space = pl.BlockSpec(memory_space=pl.ANY)
    if kind == "main":
        grid = 4
        shape = [pltpu.VMEM((2, 4, height, rows), jnp.float32)] * 2
        out_specs = [
            pl.BlockSpec((2, 1, height, rows), lambda i: (0, jnp.where(i == 1, 2, jnp.where(i == 2, 1, i)), 0, 0)),
            pl.BlockSpec((2, 1, height, rows), lambda i: (0, i, 0, 0)),
        ]
        more = [pltpu.VMEM(cot.shape, cot.dtype), pltpu.SemaphoreType.DMA]
        cot_space = pltpu.HBM
    else:
        grid = 1
        shape = [jax.ShapeDtypeStruct((2, 2, height, rows), jnp.float32)]
        out_specs = [pl.BlockSpec((2, 2, height, rows), lambda i: (0, 0, 0, 0))]
        more = []
        cot_space = pltpu.VMEM
    geom = pltpu.VMEM((harm, 2 * rows, rows), jnp.bfloat16)
    return pl.pallas_call(
        functools.partial(kernel, kind, slots, box),
        out_shape=shape,
        grid=(grid,),
        in_specs=[smem, smem, smem, smem, whole, whole, pl.BlockSpec(memory_space=cot_space), any_space],
        out_specs=out_specs,
        scratch_shapes=[
            geom,
            geom,
            pltpu.VMEM((2, 8, rows), jnp.float32),
            pltpu.SMEM((10 * tiles_max,), jnp.int32),
            pltpu.SMEM((16,), jnp.int32),
            pltpu.SMEM((3 * (2 * tiles_max + 4),), jnp.int32),
            *more,
        ],
        compiler_params=pltpu.CompilerParams(vmem_limit_bytes=24 * 1024 * 1024),
        cost_estimate=pl.CostEstimate(flops=0, bytes_accessed=0, transcendentals=0),
        name=kind,
    )(
        meta,
        pair_tile,
        pair_block,
        bounds,
        probe,
        pos,
        pltpu.with_memory_space_constraint(cot, cot_space),
        after,
    )


def join_kernel(where, back_ref, top_in, bottom_in, top_ref, bottom_ref):
    side, top, bottom = where[0], where[1], where[2]
    top_ref[side, top] = top_in[side, top] + back_ref[0]
    bottom_ref[side, bottom] = bottom_in[side, bottom] + back_ref[1]


def join(where, back, top, bottom):
    whole = pl.BlockSpec(memory_space=pltpu.VMEM)
    return pl.pallas_call(
        join_kernel,
        out_shape=[pltpu.VMEM(top.shape, top.dtype), pltpu.VMEM(bottom.shape, bottom.dtype)],
        in_specs=[pl.BlockSpec(memory_space=pltpu.SMEM), whole, whole, whole],
        out_specs=[whole, whole],
        input_output_aliases={2: 0, 3: 1},
        compiler_params=pltpu.CompilerParams(vmem_limit_bytes=4 * 1024 * 1024),
        name="join",
    )(where, back, top, bottom)


def hold_kernel(cot_hbm, probe_ref, bounds_ref, meta_ref, out_ref, token_ref, sem):
    copy = pltpu.make_async_copy(cot_hbm, out_ref, sem)
    copy.start()
    token_ref[...] = jnp.zeros_like(token_ref)
    copy.wait()


def hold(cot, probe, bounds, meta):
    any_space = pl.BlockSpec(memory_space=pl.ANY)
    whole = pl.BlockSpec(memory_space=pltpu.VMEM)
    return pl.pallas_call(
        hold_kernel,
        out_shape=[
            pltpu.VMEM(cot.shape, cot.dtype),
            jax.ShapeDtypeStruct((15, rows), jnp.float32),
        ],
        in_specs=[pl.BlockSpec(memory_space=pltpu.HBM), any_space, any_space, any_space],
        out_specs=[whole, whole],
        scratch_shapes=[pltpu.SemaphoreType.DMA],
        compiler_params=pltpu.CompilerParams(vmem_limit_bytes=2 * 1024 * 1024),
        name="hold",
    )(pltpu.with_memory_space_constraint(cot, pltpu.HBM), probe, bounds, meta)


def on_device(
    cotangent, probe_pos, atom_pos, pair_tile, pair_block, pair_count, send_left, send_right
):
    ndom = lax.axis_size("dom")
    ntile = lax.axis_size("tile")
    slab = lax.axis_index("dom")
    place = lax.axis_index("tile")
    core = place % 2
    chips = ntile // 2
    box = ndom * slab_width
    up = [(i, (i + 1) % ndom) for i in range(ndom)]
    down = [(j, i) for i, j in up]
    swap = [(i, i ^ 1) for i in range(ntile)]

    def along(o):
        return [(z * 2 + c, ((z + o) % chips) * 2 + c) for z in range(chips) for c in range(2)]

    ids = jnp.concatenate([send_left, send_right], axis=0)[:, :1].astype(jnp.float32)
    own = jnp.concatenate([atom_pos, jnp.broadcast_to(ids, (2, rows))], axis=0)
    own = lax.optimization_barrier(own)
    before = lax.ppermute(own, "dom", up)
    after = lax.ppermute(own, "dom", down)
    meta = jnp.stack([pair_count[0], place // 2, core, slab, jnp.int32(ndom)])
    shaped = (probe_pos[1] * 0.25).reshape(-1, rows)
    bounds = jnp.stack([jnp.min(shaped, axis=1), jnp.max(shaped, axis=1)])
    probe = (probe_pos * 0.25).T
    cot, token = hold(cotangent, probe, bounds, meta)
    three = jnp.concatenate([own, before, after], axis=0)
    three = three + token
    pos = three[None]
    for bit in (1, 2, 4):
        other = lax.ppermute(pos, "tile", [(i, i ^ bit) for i in range(ntile)])
        pos = jnp.concatenate([pos, other], axis=0)
    pos = pos.reshape(chips, 2, *three.shape)

    home = []
    for s in range(ndom):
        for t in range(ntile):
            way = 1 if t % 2 else -1
            home.append((s * ntile + t, ((s + way) % ndom) * ntile + t))
    lent_id = jnp.where(core == 0, send_right[0, 0], send_left[0, 0])
    away = lax.rem(lent_id // 2 - place // 2 + chips, chips)
    lent_side = jnp.where(lent_id % 2 == core, 0, 1)
    top_at = jnp.where(away == 2, 0, jnp.where(away == 1, 2, jnp.where(away == 3, 1, 3)))
    bottom_at = jnp.where(away == 2, 0, jnp.where(away == 1, 1, jnp.where(away == 3, 2, 3)))
    lent_place = jnp.stack([lent_side, top_at, bottom_at]).astype(jnp.int32)

    args = (meta, pair_tile, pair_block, bounds, probe, pos, cot, box)
    (lent,) = compute("lent", *args, atom_pos)
    lent = lent[:, 0] + lax.ppermute(lent[:, 1], "tile", swap)
    back = lax.ppermute(lent, ("dom", "tile"), home)
    top, bottom = compute("main", *args[:-2], cotangent, box, lent)
    top, bottom = join(lent_place, back, top, bottom)

    def over_cores(part, first):
        at = slice(first, first + 2)
        return part[0, at] + lax.ppermute(part[1, at], "tile", swap)

    far_top, last_top = over_cores(top, 0)
    far_bottom, next_bottom = over_cores(bottom, 0)
    far_ahead = lax.ppermute(far_top, "tile", along(1))
    far_behind = lax.ppermute(far_bottom, "tile", along(-1))
    near_behind = lax.ppermute(last_top, "tile", along(-1))
    near_ahead = lax.ppermute(next_bottom, "tile", along(1))
    next_top, here_top = over_cores(top, 2)
    last_bottom, here_bottom = over_cores(bottom, 2)
    ahead, behind, near_ahead, near_behind = lax.optimization_barrier(
        (next_top + far_ahead, last_bottom + far_behind, near_ahead, near_behind)
    )
    end_ahead = lax.ppermute(ahead, "tile", along(1))
    end_behind = lax.ppermute(behind, "tile", along(-1))
    halves = (here_top + near_behind + end_ahead, here_bottom + near_ahead + end_behind)
    shape = (cotangent.shape[0], -1, rows)
    total = jnp.concatenate([h.astype(jnp.bfloat16).reshape(shape) for h in halves], axis=1)
    return total


def solution(mesh):
    placed = (
        P(None, None, ("dom", "tile")),
        P(None, ("dom", "tile")),
        P(None, ("dom", "tile")),
        P(("dom", "tile")),
        P(("dom", "tile")),
        P(("dom", "tile")),
        P("dom", None),
        P("dom", None),
    )
    return jax.shard_map(
        on_device,
        mesh=mesh,
        in_specs=placed,
        out_specs=P(None, None, ("dom", "tile")),
        check_vma=False,
    )
```

```python
import functools

import jax
import jax.numpy as jnp
from jax import lax
from jax.experimental import pallas as pl
from jax.experimental.pallas import tpu as pltpu
from jax.sharding import PartitionSpec as P

cutoff = 4.0
slab_width = 5.0
rows = 128
offsets = (2, 1, 3, 0)
tiles_max = 20
every = tuple(range(25))


def harmonics(e, x, y, z, xx, yy, zz, wanted):
    rr = xx + yy + zz
    ex = e * x
    ey = e * y
    ez = e * z
    exy = ex * y
    eyz = ey * z
    exz = ex * z
    d = xx - yy
    ed = e * d
    z3 = 3.0 * zz
    z5 = 5.0 * zz
    z7 = 7.0 * zz
    r3 = 3.0 * rr
    f = 3.0 * xx - yy
    k = xx - 3.0 * yy
    g = z5 - rr
    h = z5 - r3
    w = z7 - rr
    v = z7 - r3
    made = {
        0: lambda: e,
        1: lambda: 2.0 * ex,
        2: lambda: 2.0 * ey,
        3: lambda: 2.0 * ez,
        4: lambda: 3.0 * exy,
        5: lambda: 3.0 * eyz,
        6: lambda: (1.5 * e) * (z3 - rr),
        7: lambda: 3.0 * exz,
        8: lambda: 1.5 * ed,
        9: lambda: (5.0 * ey) * f,
        10: lambda: 10.0 * (exy * z),
        11: lambda: (5.0 * ey) * g,
        12: lambda: (5.0 * ez) * h,
        13: lambda: (5.0 * ex) * g,
        14: lambda: (5.0 * ez) * d,
        15: lambda: (5.0 * ex) * k,
        16: lambda: (8.0 * exy) * d,
        17: lambda: (8.0 * eyz) * f,
        18: lambda: (8.0 * exy) * w,
        19: lambda: (8.0 * eyz) * v,
        20: lambda: e * (z5 * (z7 - 6.0 * rr) + r3 * rr),
        21: lambda: (8.0 * exz) * v,
        22: lambda: (4.0 * ed) * w,
        23: lambda: (8.0 * exz) * k,
        24: lambda: (2.0 * e) * (xx * k - yy * f),
    }
    return [made[m]() for m in wanted]


far = 1000.0
chunk = 16


def geometry(tile, r, atom, probe_ref):
    p = probe_ref[pl.ds(pl.multiple_of(tile * rows + r * chunk, chunk), chunk), :]
    x = p[:, 0:1] - atom[0]
    y = p[:, 1:2] - atom[1]
    z = p[:, 2:3] - atom[2]
    xx = x * x
    yy = y * y
    zz = z * z
    inside = jnp.maximum(1.0 - (xx + yy + zz), 0.0)
    return harmonics(inside * inside, x, y, z, xx, yy, zz, every)


def add_term(m, side, tiles, cot_ref, geom, top_ref, bottom_ref):
    piece = jnp.concatenate(
        [cot_ref[m, :, pl.ds(pl.multiple_of(tile * rows, rows), rows)] for tile in tiles], axis=1
    )
    term = jnp.dot(piece, geom[m], preferred_element_type=jnp.float32)
    half = term.shape[0] // 2
    at = slice(m * half, m * half + half)
    top_ref[side, at, :] = top_ref[side, at, :] + term[:half]
    bottom_ref[side, at, :] = bottom_ref[side, at, :] + term[half:]


def make_and_add(make, add, atoms, probe_ref, cot_ref, made, used, outs):
    chunks = [(n, r) for n in range(2) for r in range(rows // chunk)] if make else []
    turns = len(chunks) or 1
    for turn in range(turns):
        if make:
            n, r = chunks[turn]
            values = geometry(make[n], r, atoms[n], probe_ref)
            at = slice(n * rows + r * chunk, n * rows + r * chunk + chunk)
            for m, value in enumerate(values):
                made[m, at, :] = value.astype(jnp.bfloat16)
        if add:
            side, tiles = add
            for m in range(turn * len(every) // turns, (turn + 1) * len(every) // turns):
                add_term(m, side, tiles, cot_ref, used, *outs)


def fill_lists(slots, tile_ref, block_ref, count, lists, counts):
    def clear(b, carry):
        counts[b] = 0
        return carry

    lax.fori_loop(0, 10, clear, 0)

    def put(j, carry):
        b = block_ref[j]
        n = counts[b]
        lists[b * tiles_max + n] = tile_ref[j]
        counts[b] = n + 1
        return carry

    lax.fori_loop(0, jnp.minimum(count, slots), put, 0)


def list_steps(side, b, atom, bounds, lists, counts, steps, n):
    ymin = jnp.min(atom[1])
    ymax = jnp.max(atom[1])

    def keep(j, found):
        tile = lists[b * tiles_max + j]
        gap = jnp.maximum(ymin - bounds[1, tile], bounds[0, tile] - ymax)
        near = gap < 1.0
        at = 3 * n + 3 * (found // 2)
        odd = found % 2

        @pl.when(near)
        def _():
            steps[at] = side
            steps[at + 1 + odd] = tile

            @pl.when(odd == 0)
            def _():
                steps[at + 2] = -1

        return found + jnp.where(near, 1, 0)

    return n + (lax.fori_loop(0, counts[b], keep, 0) + 1) // 2


def kernel(kind, slots, box, meta, tile_ref, block_ref, bounds, probe_ref, pos_ref, cot_ref, after_ref, *rest):
    *outs, first_geom, second_geom, atom_ref, lists, counts, steps = rest[: len(rest) - 2 * (kind == "main")]
    step = pl.program_id(0)
    if kind == "main":
        held, sem = rest[-2:]
        copy = pltpu.make_async_copy(cot_ref, held, sem)
        cot_ref = held

    @pl.when(step == 0)
    def _():
        if kind == "main":
            copy.start()
        fill_lists(slots, tile_ref, block_ref, meta[0], lists, counts)

    core = meta[2]
    if kind == "main":
        halves = [ref.at[:, 0] for ref in outs]
    else:
        halves = [outs[0].at[0], outs[0].at[1]]
    for ref in halves:
        ref[...] = jnp.zeros(ref.shape, jnp.float32)
    n = 0
    for side in range(2):
        if kind == "main":
            offset = jnp.where(step == 0, 2, jnp.where(step == 1, 1, jnp.where(step == 2, 3, 0)))
            chip = lax.rem(meta[1] + offset, 4)
            b = chip * 2 + (core if side == 0 else 1 - core)
            place = lax.bitwise_xor(chip, meta[1])
            atom = [pos_ref[place, side, i : i + 1, :] for i in range(3)]
        else:
            which = core if side == 0 else 1 - core
            b = 8 + which
            lent_left = jnp.max(pos_ref[0, 0, 9:10, :])
            lent_right = jnp.max(pos_ref[0, 0, 13:14, :])
            source = jnp.where(which == 0, lent_left, lent_right).astype(jnp.int32)
            place = lax.bitwise_xor(source // 2, meta[1])
            other = jnp.where(lax.rem(source, 2) == core, 0, 1)
            left = [pos_ref[place, other, 5 + i : 6 + i, :] for i in range(3)]
            right = [pos_ref[place, other, 10 + i : 11 + i, :] for i in range(3)]
            left[0] = left[0] + jnp.where(meta[3] == 0, -box, 0.0)
            right[0] = right[0] + jnp.where(meta[3] == meta[4] - 1, box, 0.0)
            atom = [jnp.where(which == 0, l, r) for l, r in zip(left, right)]
        atom = [a * 0.25 for a in atom]
        for i in range(3):
            atom_ref[side, i : i + 1, :] = atom[i]
        n = list_steps(side, b, atom, bounds, lists, counts, steps, n)

    def one(j):
        side, first, second = steps[3 * j], steps[3 * j + 1], steps[3 * j + 2]
        atom = [atom_ref[side, i : i + 1, :] for i in range(3)]
        moved = [atom[0] - jnp.where(second < 0, far, 0.0), *atom[1:]]
        return side, (first, jnp.maximum(second, 0)), (atom, moved)

    def turn(make, add, made, used):
        made_step = one(make) if make is not None else (None, None, None)
        added = one(add)[:2] if add is not None else None
        make_and_add(made_step[1], added, made_step[2], probe_ref, cot_ref, made, used, halves)

    @pl.when(n > 0)
    def _():
        turn(0, None, first_geom, None)

    if kind == "main":
        pl.when(step == 0)(copy.wait)

    def both(k, carry):
        turn(2 * k + 1, 2 * k, second_geom, first_geom)
        turn(2 * k + 2, 2 * k + 1, first_geom, second_geom)
        return carry

    whole = jnp.maximum(n - 1, 0) // 2
    lax.fori_loop(0, whole, both, 0)

    @pl.when(n - 2 * whole == 1)
    def _():
        turn(None, n - 1, None, first_geom)

    @pl.when(n - 2 * whole == 2)
    def _():
        turn(n - 1, n - 2, second_geom, first_geom)
        turn(None, n - 1, None, second_geom)


def compute(kind, meta, pair_tile, pair_block, bounds, probe, pos, cot, box, after):
    harm, chan, width = cot.shape
    height = harm * chan // 2
    slots = pair_tile.shape[0]
    smem = pl.BlockSpec(memory_space=pltpu.SMEM)
    whole = pl.BlockSpec(memory_space=pltpu.VMEM)
    any_space = pl.BlockSpec(memory_space=pl.ANY)
    if kind == "main":
        grid = 4
        shape = [pltpu.VMEM((2, 4, height, rows), jnp.float32)] * 2
        out_specs = [
            pl.BlockSpec((2, 1, height, rows), lambda i: (0, jnp.where(i == 1, 2, jnp.where(i == 2, 1, i)), 0, 0)),
            pl.BlockSpec((2, 1, height, rows), lambda i: (0, i, 0, 0)),
        ]
        more = [pltpu.VMEM(cot.shape, cot.dtype), pltpu.SemaphoreType.DMA]
        cot_space = pltpu.HBM
    else:
        grid = 1
        shape = [jax.ShapeDtypeStruct((2, 2, height, rows), jnp.float32)]
        out_specs = [pl.BlockSpec((2, 2, height, rows), lambda i: (0, 0, 0, 0))]
        more = []
        cot_space = pltpu.VMEM
    geom = pltpu.VMEM((harm, 2 * rows, rows), jnp.bfloat16)
    return pl.pallas_call(
        functools.partial(kernel, kind, slots, box),
        out_shape=shape,
        grid=(grid,),
        in_specs=[smem, smem, smem, smem, whole, whole, pl.BlockSpec(memory_space=cot_space), any_space],
        out_specs=out_specs,
        scratch_shapes=[
            geom,
            geom,
            pltpu.VMEM((2, 8, rows), jnp.float32),
            pltpu.SMEM((10 * tiles_max,), jnp.int32),
            pltpu.SMEM((16,), jnp.int32),
            pltpu.SMEM((3 * (2 * tiles_max + 4),), jnp.int32),
            *more,
        ],
        compiler_params=pltpu.CompilerParams(vmem_limit_bytes=24 * 1024 * 1024),
        cost_estimate=pl.CostEstimate(flops=0, bytes_accessed=0, transcendentals=0),
        name=kind,
    )(
        meta,
        pair_tile,
        pair_block,
        bounds,
        probe,
        pos,
        pltpu.with_memory_space_constraint(cot, cot_space),
        after,
    )


def join_kernel(where, back_ref, top_in, bottom_in, top_ref, bottom_ref):
    side, top, bottom = where[0], where[1], where[2]
    top_ref[side, top] = top_in[side, top] + back_ref[0]
    bottom_ref[side, bottom] = bottom_in[side, bottom] + back_ref[1]


def join(where, back, top, bottom):
    whole = pl.BlockSpec(memory_space=pltpu.VMEM)
    return pl.pallas_call(
        join_kernel,
        out_shape=[pltpu.VMEM(top.shape, top.dtype), pltpu.VMEM(bottom.shape, bottom.dtype)],
        in_specs=[pl.BlockSpec(memory_space=pltpu.SMEM), whole, whole, whole],
        out_specs=[whole, whole],
        input_output_aliases={2: 0, 3: 1},
        compiler_params=pltpu.CompilerParams(vmem_limit_bytes=4 * 1024 * 1024),
        name="join",
    )(where, back, top, bottom)


def hold_kernel(cot_hbm, probe_ref, bounds_ref, meta_ref, out_ref, token_ref, sem):
    copy = pltpu.make_async_copy(cot_hbm, out_ref, sem)
    copy.start()
    token_ref[...] = jnp.zeros_like(token_ref)
    copy.wait()


def hold(cot, probe, bounds, meta):
    any_space = pl.BlockSpec(memory_space=pl.ANY)
    whole = pl.BlockSpec(memory_space=pltpu.VMEM)
    return pl.pallas_call(
        hold_kernel,
        out_shape=[
            pltpu.VMEM(cot.shape, cot.dtype),
            jax.ShapeDtypeStruct((15, rows), jnp.float32),
        ],
        in_specs=[pl.BlockSpec(memory_space=pltpu.HBM), any_space, any_space, any_space],
        out_specs=[whole, whole],
        scratch_shapes=[pltpu.SemaphoreType.DMA],
        compiler_params=pltpu.CompilerParams(vmem_limit_bytes=2 * 1024 * 1024),
        name="hold",
    )(pltpu.with_memory_space_constraint(cot, pltpu.HBM), probe, bounds, meta)


def on_device(
    cotangent, probe_pos, atom_pos, pair_tile, pair_block, pair_count, send_left, send_right
):
    ndom = lax.axis_size("dom")
    ntile = lax.axis_size("tile")
    slab = lax.axis_index("dom")
    place = lax.axis_index("tile")
    core = place % 2
    chips = ntile // 2
    box = ndom * slab_width
    up = [(i, (i + 1) % ndom) for i in range(ndom)]
    down = [(j, i) for i, j in up]
    swap = [(i, i ^ 1) for i in range(ntile)]

    def along(o):
        return [(z * 2 + c, ((z + o) % chips) * 2 + c) for z in range(chips) for c in range(2)]

    ids = jnp.concatenate([send_left, send_right], axis=0)[:, :1].astype(jnp.float32)
    own = jnp.concatenate([atom_pos, jnp.broadcast_to(ids, (2, rows))], axis=0)
    own = lax.optimization_barrier(own)
    before = lax.ppermute(own, "dom", up)
    after = lax.ppermute(own, "dom", down)
    meta = jnp.stack([pair_count[0], place // 2, core, slab, jnp.int32(ndom)])
    shaped = (probe_pos[1] * 0.25).reshape(-1, rows)
    bounds = jnp.stack([jnp.min(shaped, axis=1), jnp.max(shaped, axis=1)])
    probe = (probe_pos * 0.25).T
    cot, token = hold(cotangent, probe, bounds, meta)
    three = jnp.concatenate([own, before, after], axis=0)
    three = three + token
    pos = three[None]
    for bit in (1, 2, 4):
        other = lax.ppermute(pos, "tile", [(i, i ^ bit) for i in range(ntile)])
        pos = jnp.concatenate([pos, other], axis=0)
    pos = pos.reshape(chips, 2, *three.shape)

    home = []
    for s in range(ndom):
        for t in range(ntile):
            way = 1 if t % 2 else -1
            home.append((s * ntile + t, ((s + way) % ndom) * ntile + t))
    lent_id = jnp.where(core == 0, send_right[0, 0], send_left[0, 0])
    away = lax.rem(lent_id // 2 - place // 2 + chips, chips)
    lent_side = jnp.where(lent_id % 2 == core, 0, 1)
    top_at = jnp.where(away == 2, 0, jnp.where(away == 1, 2, jnp.where(away == 3, 1, 3)))
    bottom_at = jnp.where(away == 2, 0, jnp.where(away == 1, 1, jnp.where(away == 3, 2, 3)))
    lent_place = jnp.stack([lent_side, top_at, bottom_at]).astype(jnp.int32)

    args = (meta, pair_tile, pair_block, bounds, probe, pos, cot, box)
    (lent,) = compute("lent", *args, atom_pos)
    lent = lent[:, 0] + lax.ppermute(lent[:, 1], "tile", swap)
    back = lax.ppermute(lent, ("dom", "tile"), home)
    top, bottom = compute("main", *args[:-2], cotangent, box, lent)
    top, bottom = join(lent_place, back, top, bottom)

    def over_cores(part, first):
        at = slice(first, first + 2)
        return part[0, at] + lax.ppermute(part[1, at], "tile", swap)

    far_top, last_top = over_cores(top, 0)
    far_bottom, next_bottom = over_cores(bottom, 0)
    send_top, far_top = lax.optimization_barrier((top[1, 2:4], far_top))
    send_bottom, far_bottom = lax.optimization_barrier((bottom[1, 2:4], far_bottom))
    next_top, here_top = top[0, 2:4] + lax.ppermute(send_top, "tile", swap)
    last_bottom, here_bottom = bottom[0, 2:4] + lax.ppermute(send_bottom, "tile", swap)
    far_ahead = lax.ppermute(far_top, "tile", along(1))
    far_behind = lax.ppermute(far_bottom, "tile", along(-1))
    near_behind = lax.ppermute(last_top, "tile", along(-1))
    near_ahead = lax.ppermute(next_bottom, "tile", along(1))
    ahead, behind, near_ahead, near_behind = lax.optimization_barrier(
        (next_top + far_ahead, last_bottom + far_behind, near_ahead, near_behind)
    )
    end_ahead = lax.ppermute(ahead, "tile", along(1))
    end_behind = lax.ppermute(behind, "tile", along(-1))
    halves = (here_top + near_behind + end_ahead, here_bottom + near_ahead + end_behind)
    shape = (cotangent.shape[0], -1, rows)
    total = jnp.concatenate([h.astype(jnp.bfloat16).reshape(shape) for h in halves], axis=1)
    return total


def solution(mesh):
    placed = (
        P(None, None, ("dom", "tile")),
        P(None, ("dom", "tile")),
        P(None, ("dom", "tile")),
        P(("dom", "tile")),
        P(("dom", "tile")),
        P(("dom", "tile")),
        P("dom", None),
        P("dom", None),
    )
    return jax.shard_map(
        on_device,
        mesh=mesh,
        in_specs=placed,
        out_specs=P(None, None, ("dom", "tile")),
        check_vma=False,
    )
```
